256 devices in a mesh: dp: 64 (over z, x, core), tp: 4 (over y).
Axes of the slice: x: 4, y: 4, z: 8, core: 2. Of those that a mesh axis runs over, the one named last changes fastest.
Arguments:
- hidden: bfloat16 [2048, 4096], P('dp', 'tp'), may hold values from -6 to 6
- routes: int32 [2048, 8], P('dp'), may hold values from 0 to 63, all different within a row; in each aligned block of 32 rows (0 to 31, 32 to 63, ...) at most 8 rows name the same one
- routing_weights: float32 [2048, 8], P('dp'), may hold values from 0.05 to 1
- w_gate: bfloat16 [64, 4096, 1536], P('dp', None, 'tp'), may hold values from -0.09375 to 0.09375
- w_up: bfloat16 [64, 4096, 1536], P('dp', None, 'tp'), may hold values from -0.09375 to 0.09375
- w_down: bfloat16 [64, 1536, 4096], P('dp', 'tp'), may hold values from -0.15625 to 0.15625
- norm_gain: float32 [4096], replicated, may hold values from 0.1 to 1.9
- key_projection_weight: bfloat16 [4096, 512], P(None, 'tp'), may hold values from -0.09375 to 0.09375
- value_projection_weight: bfloat16 [4096, 512], P(None, 'tp'), may hold values from -0.09375 to 0.09375
- queries: bfloat16 [2048, 8192], P('dp', 'tp'), may hold values from -128 to 128
- cached_key_rows: bfloat16 [64, 128, 512], P('dp', None, 'tp'), may hold values from -4 to 4
- cached_value_rows: bfloat16 [64, 128, 512], P('dp', None, 'tp'), may hold values from -6 to 6
- lengths: int32 [64], P('dp'), may hold values from 16 to 128
- parents: int32 [64, 32], P('dp'), may hold values from -1 to 30, as said below
Outputs:
- layer_output: bfloat16 [2048, 4096], P('dp', 'tp')
- next_layer_keys: bfloat16 [2048, 512], P('dp', 'tp')
- next_layer_values: bfloat16 [2048, 512], P('dp', 'tp')
- attended: bfloat16 [2048, 8192], P('dp', 'tp')
The draws below stay inside these ranges and needn't reach their ends.
Inputs may be any that keep to these rules, and one draw needn't show every extreme that they name: `routes`: each row names 8 different experts. In each aligned block of 32 rows (the rows of one device) no expert is named by more than 8 rows, a bound that some block reaches. `parents`: node 0 of each request is the root, with parent -1; every other node i has its parent among nodes max(0, i - 8) to i - 1.
All inputs are finite; a program needn't handle non-finite values.
Results may differ from the reference program's by a relative error of at most 0.013.
Values may be sent and summed in bfloat16 or wider, within the bound.
No kernel may reach another device: no remote copies, remote signals or barrier semaphores. Data moves between devices by JAX's collectives and lax.ppermute only.
A program may use at most 64 MiB of HBM per device.

```python
import math
import jax
import jax.numpy as jnp
import numpy as np
from jax import lax

MODEL_WIDTH = 4096
QUERY_HEADS = 64
KEY_VALUE_HEADS = 4
HEAD_SIZE = 128
FF = 1536
TOP = 8
TREE_TOKENS = 32
CONTEXT_SLOTS = 128
EXPERTS = 64
T_DEV = 32
REQUEST_TOTAL = 64
TOKENS = 2048
CAP = 8
N_DP = 64
N_TP = 4


def attention_pair(key):
    request_key_cache = jax.random.fold_in(key, 101)
    key_query = jax.random.fold_in(key, 202)
    kept_length = jnp.clip(jax.random.normal(request_key_cache, (REQUEST_TOTAL, CONTEXT_SLOTS, KEY_VALUE_HEADS, HEAD_SIZE), jnp.float32), -4.0, 4.0)
    wanted_rows = jnp.clip(jax.random.normal(key_query, (REQUEST_TOTAL, TREE_TOKENS, QUERY_HEADS, HEAD_SIZE), jnp.float32), -4.0, 4.0)
    return (kept_length.reshape(REQUEST_TOTAL, CONTEXT_SLOTS, KEY_VALUE_HEADS * HEAD_SIZE), wanted_rows.reshape(REQUEST_TOTAL * TREE_TOKENS, QUERY_HEADS * HEAD_SIZE))


def draw_queries(key, part):
    return attention_pair(key)[1].astype(jnp.bfloat16)


def draw_cached_key_rows(key, part):
    return attention_pair(key)[0].astype(jnp.bfloat16)


def draw_parents(key, part):
    position = jnp.arange(TREE_TOKENS, dtype=jnp.int32)
    lowest = jnp.maximum(position - 8, 0)
    highest = jnp.maximum(position, 1)
    picks = jax.random.randint(jax.random.fold_in(key, 303), (REQUEST_TOTAL, TREE_TOKENS), lowest, highest, dtype=jnp.int32)
    return jnp.where(position[None, :] == 0, -1, picks).astype(jnp.int32)


def set_ends(values, own_key, low, top_value):
    longest = values.shape.index(max(values.shape))
    spots = []
    for shift in (0, 1):
        where = [jax.random.randint(jax.random.fold_in(own_key, axis), (), 0, length) for axis, length in enumerate(values.shape)]
        where[longest] = (where[longest] + shift) % values.shape[longest]
        spots.append(tuple(where))
    return values.at[spots[0]].set(low).at[spots[1]].set(top_value)


def level_of(key, extent, split, smallest, high):
    loudness, own = 1.0, jax.random.fold_in(key, 6)
    for dim, blocks in split:
        heights = jnp.exp(jax.random.uniform(jax.random.fold_in(own, dim), (blocks,), jnp.float32, smallest / len(split), high / len(split)))
        loudness = loudness * jnp.repeat(heights, extent[dim] // blocks).reshape([-1 if axis == dim else 1 for axis in range(len(extent))])
    return loudness


def routed_block(key, own, number, rows, amount, top, bound, skew):
    ranking = jax.random.permutation(key, amount)
    heavy_load, usual = portions_of(amount, rows * top, bound, skew, True), portions_of(amount, rows * top, bound, skew, False)
    places = jnp.arange(amount)

    def named(sizes, turn):
        used = int((sizes > 0).sum())
        fixed = max(1, used // 4)
        shifted = fixed + (places - fixed + turn * (used - fixed)) % max(1, amount - fixed)
        return jnp.zeros((amount,), jnp.int32).at[ranking[jnp.where(places < fixed, places, shifted)]].set(jnp.asarray(sizes, jnp.int32))

    sizes = jnp.where(number % 4 == 0, named(heavy_load, number // 4), named(usual, number - number // 4 - 1))
    mixed = jax.random.permutation(jax.random.fold_in(own, 3), amount)
    source_of, taker = mixed[0:amount // 2 * 2:2], mixed[1:amount // 2 * 2:2]
    slack = jnp.minimum(sizes[source_of] - 1, bound - sizes[taker]) // 2
    slack = jnp.where((source_of == ranking[0]) | (taker == ranking[0]) | (sizes[taker] == 0), 0, jnp.maximum(slack, 0))
    shifted = jax.random.randint(jax.random.fold_in(own, 4), (amount // 2,), 0, 1 << 20) % (slack + 1)
    sizes = sizes.at[source_of].add(-shifted).at[taker].add(shifted)
    labels = jnp.searchsorted(jnp.cumsum(sizes), jnp.arange(rows * top), side="right").astype(jnp.int32)
    grid = labels.reshape(top, rows).T
    grid = grid[jax.random.permutation(jax.random.fold_in(own, 1), rows)]
    turn = jax.random.randint(jax.random.fold_in(own, 2), (rows, 1), 0, top)
    return jnp.take_along_axis(grid, (jnp.arange(top)[None, :] + turn) % top, axis=1)


def portions_of(number_of, total, reach, slope, full):
    weights = [(1 << 20) // math.isqrt(grade ** slope) + 1 for grade in range(1, number_of + 1)]
    largest = reach if full else min(reach, max(-(-total // number_of), total * weights[0] // sum(weights)))
    least = 1 if total - largest >= number_of - 1 else 0
    given, spare = [largest] + [least] * (number_of - 1), total - largest - least * (number_of - 1)
    while spare > 0:
        free = [i for i in range(1, number_of) if given[i] < largest] or [i for i in range(1, number_of) if given[i] < reach]
        pool, budget = sum([weights[i] for i in free]), spare
        for i in free:
            extra = min(reach - given[i], max(1, budget * weights[i] // pool), spare)
            given[i] = given[i] + extra
            spare = spare - extra
    return np.array(given)


def noise(key, shape, scale, most, split=(), kind=jnp.bfloat16):
    drawn = scale * jax.random.normal(key, shape, jnp.float32)
    if split:
        drawn = drawn * level_of(key, shape, split, -0.22, 0.18)
    return jnp.clip(drawn, -most, most).astype(kind)


def setup_inputs(seed: int = 0) -> dict:
    key_of = jax.random.split(jax.random.key(seed), 15)
    hidden = noise(key_of[0], (TOKENS, MODEL_WIDTH), 1.0, 6.0, ((0, 64), (1, 4)))
    routes_keys = jax.random.split(jax.random.fold_in(key_of[1], 1), TOKENS // T_DEV)
    routes_turns = jax.random.permutation(jax.random.fold_in(key_of[1], 3), TOKENS // T_DEV)
    routes = jax.vmap(lambda own, number: routed_block(jax.random.fold_in(key_of[1], 2), own, number, T_DEV, EXPERTS, TOP, CAP, 2))(routes_keys, routes_turns).reshape((TOKENS, TOP))
    routing_weights = jnp.clip(jnp.exp(math.log(1.0) - 2.9957323 * jax.random.uniform(key_of[2], (TOKENS, TOP), jnp.float32) ** level_of(key_of[2], (TOKENS, TOP), ((0, 64),), -0.2, 0.2)), 0.05, 1.0)
    w_gate = noise(key_of[3], (EXPERTS, MODEL_WIDTH, FF), MODEL_WIDTH ** -0.5, 0.09375, ((0, 64), (2, 4)))
    w_up = noise(key_of[4], (EXPERTS, MODEL_WIDTH, FF), MODEL_WIDTH ** -0.5, 0.09375, ((0, 64), (2, 4)))
    w_down = noise(key_of[5], (EXPERTS, FF, MODEL_WIDTH), FF ** -0.5, 0.15625, ((0, 64), (1, 4)))
    norm_gain = jnp.clip(1.0 + 0.18 * jax.random.normal(key_of[6], (MODEL_WIDTH,), jnp.float32), 0.1, 1.9)
    key_projection_weight = noise(key_of[7], (MODEL_WIDTH, KEY_VALUE_HEADS * HEAD_SIZE), MODEL_WIDTH ** -0.5, 0.09375, ((1, 4),))
    value_projection_weight = noise(key_of[8], (MODEL_WIDTH, KEY_VALUE_HEADS * HEAD_SIZE), MODEL_WIDTH ** -0.5, 0.09375, ((1, 4),))
    queries = draw_queries(jax.random.fold_in(key_of[14], 71), 0)
    cached_key_rows = draw_cached_key_rows(jax.random.fold_in(key_of[14], 71), 0)
    cached_value_rows = noise(key_of[11], (REQUEST_TOTAL, CONTEXT_SLOTS, KEY_VALUE_HEADS * HEAD_SIZE), 1.0, 6.0, ((0, 64), (2, 4)))
    lengths = set_ends(jax.random.randint(key_of[12], (REQUEST_TOTAL,), max(2, CONTEXT_SLOTS // 8), CONTEXT_SLOTS + 1), jax.random.fold_in(key_of[12], 1), max(2, CONTEXT_SLOTS // 8), CONTEXT_SLOTS).astype(jnp.int32)
    parents = draw_parents(jax.random.fold_in(key_of[14], 71), 0)
    return {"hidden": hidden, "routes": routes, "routing_weights": routing_weights, "w_gate": w_gate, "w_up": w_up, "w_down": w_down, "norm_gain": norm_gain, "key_projection_weight": key_projection_weight, "value_projection_weight": value_projection_weight, "queries": queries, "cached_key_rows": cached_key_rows, "cached_value_rows": cached_value_rows, "lengths": lengths, "parents": parents}


def ancestry(parent_row):
    node_count = parent_row.shape[0]
    position = jnp.arange(node_count, dtype=jnp.int32)
    reached = (parent_row[:, None] == position[None, :]).astype(jnp.float32)
    reached = reached + jnp.eye(node_count, dtype=jnp.float32)
    for doubling in range((node_count - 1).bit_length()):
        reached = jnp.minimum(jnp.dot(reached, reached, preferred_element_type=jnp.float32), 1.0)
    return reached > 0.5

def request_attention(inputs):
    request_query_rows, request_key_cache, request_value_cache, tree_key_rows, tree_value_rows, length, parent_row = inputs
    query_group_count = QUERY_HEADS // KEY_VALUE_HEADS
    scaled = 1.0 / math.sqrt(HEAD_SIZE)
    highest_precision = lax.Precision.HIGHEST
    tree_query_block = request_query_rows.astype(jnp.float32).reshape(TREE_TOKENS, KEY_VALUE_HEADS, query_group_count, HEAD_SIZE)
    joined_key_block = request_key_cache.astype(jnp.float32).reshape(CONTEXT_SLOTS, KEY_VALUE_HEADS, HEAD_SIZE)
    joined_value_block = request_value_cache.astype(jnp.float32).reshape(CONTEXT_SLOTS, KEY_VALUE_HEADS, HEAD_SIZE)
    tree_key_block = tree_key_rows.astype(jnp.float32).reshape(TREE_TOKENS, KEY_VALUE_HEADS, HEAD_SIZE)
    tree_value_block = tree_value_rows.astype(jnp.float32).reshape(TREE_TOKENS, KEY_VALUE_HEADS, HEAD_SIZE)
    cache_scores = jnp.einsum('nkgd,pkd->kgnp', tree_query_block, joined_key_block, precision=highest_precision) * scaled
    tree_scores = jnp.einsum('nkgd,mkd->kgnm', tree_query_block, tree_key_block, precision=highest_precision) * scaled
    visible = jnp.arange(CONTEXT_SLOTS, dtype=jnp.int32) < length
    cache_scores = jnp.where(visible[None, None, None, :], cache_scores, -1e+30)
    tree_scores = jnp.where(ancestry(parent_row)[None, None], tree_scores, -1e+30)
    scores = jnp.concatenate([cache_scores, tree_scores], axis=-1)
    highest = lax.optimization_barrier(jnp.max(scores, axis=-1, keepdims=True))
    raised = jnp.exp(scores - highest)
    soft_weights = (raised / lax.optimization_barrier(jnp.sum(raised, axis=-1, keepdims=True))).astype(jnp.bfloat16)
    soft_weights = lax.optimization_barrier(soft_weights).astype(jnp.float32)
    output = jnp.einsum('kgnp,pkd->nkgd', soft_weights[..., :CONTEXT_SLOTS], joined_value_block, precision=highest_precision)
    output = output + jnp.einsum('kgnm,mkd->nkgd', soft_weights[..., CONTEXT_SLOTS:], tree_value_block, precision=highest_precision)
    return output.reshape(TREE_TOKENS, QUERY_HEADS * HEAD_SIZE).astype(jnp.bfloat16)

def reference(hidden, routes, routing_weights, w_gate, w_up, w_down, norm_gain, key_projection_weight, value_projection_weight, queries, cached_key_rows, cached_value_rows, lengths, parents):
    weights = routing_weights / lax.optimization_barrier(jnp.sum(routing_weights, axis=1, keepdims=True))
    slot_total = N_DP * CAP
    padded = jnp.concatenate([hidden, jnp.zeros((1, MODEL_WIDTH), hidden.dtype)], axis=0)

    def one_expert(carried, expert):
        chosen = routes == expert
        picked = jnp.any(chosen, axis=1)
        portion = lax.optimization_barrier(jnp.sum(jnp.where(chosen, weights, 0.0), axis=1))
        members = jnp.nonzero(picked, size=slot_total, fill_value=TOKENS)[0].astype(jnp.int32)
        rows_in = jnp.take(padded, members, axis=0)
        gate_act = jnp.dot(rows_in, w_gate[expert], preferred_element_type=jnp.float32)
        upward = jnp.dot(rows_in, w_up[expert], preferred_element_type=jnp.float32)
        active = (jax.nn.silu(gate_act) * upward).astype(jnp.bfloat16)
        active = lax.optimization_barrier(active)
        pieces = active.astype(jnp.float32).reshape(slot_total, N_TP, FF // N_TP)
        down_rows = w_down[expert].astype(jnp.float32).reshape(N_TP, FF // N_TP, MODEL_WIDTH)
        partial_value = jnp.einsum('snf,nfd->nsd', pieces, down_rows, precision=lax.Precision.HIGHEST).astype(jnp.bfloat16)
        partial_value = lax.optimization_barrier(partial_value)
        summed = lax.optimization_barrier(jnp.sum(partial_value.astype(jnp.float32), axis=0))
        factor = jnp.take(jnp.concatenate([portion, jnp.zeros((1,), portion.dtype)]), members)
        carried = carried.at[members].add(factor[:, None] * summed, mode='drop')
        return (carried, None)
    expert_mix, unused = lax.scan(one_expert, jnp.zeros((TOKENS, MODEL_WIDTH), jnp.float32), jnp.arange(EXPERTS, dtype=jnp.int32))
    layer_output = (hidden.astype(jnp.float32) + expert_mix).astype(jnp.bfloat16)
    widened = layer_output.astype(jnp.float32)
    scaling = lax.rsqrt(lax.optimization_barrier(jnp.mean(widened * widened, axis=1, keepdims=True)) + 1e-06)
    normed = (widened * scaling * norm_gain).astype(jnp.bfloat16)
    next_layer_keys = jnp.dot(normed, key_projection_weight, preferred_element_type=jnp.float32).astype(jnp.bfloat16)
    next_layer_values = jnp.dot(normed, value_projection_weight, preferred_element_type=jnp.float32).astype(jnp.bfloat16)
    attended = lax.map(request_attention, (queries.reshape(REQUEST_TOTAL, TREE_TOKENS, QUERY_HEADS * HEAD_SIZE), cached_key_rows, cached_value_rows, next_layer_keys.reshape(REQUEST_TOTAL, TREE_TOKENS, KEY_VALUE_HEADS * HEAD_SIZE), next_layer_values.reshape(REQUEST_TOTAL, TREE_TOKENS, KEY_VALUE_HEADS * HEAD_SIZE), lengths, parents))
    return (layer_output, next_layer_keys, next_layer_values, attended.reshape(TOKENS, QUERY_HEADS * HEAD_SIZE))
```

```python
import math

import jax
import jax.numpy as jnp
from jax import lax
from jax.sharding import PartitionSpec as P

HEAD_SIZE = 128


def split_up(shard, dim, size):
    shape = shard.shape
    tiles = shard.reshape(*shape[:dim], size, shape[dim] // size, *shape[dim + 1 :])
    return jnp.moveaxis(tiles, dim, 0)


def sent_and_summed(shard, axis, dim):
    size = lax.axis_size(axis)
    tiles = lax.all_to_all(split_up(shard, dim, size), axis, 0, 0, tiled=True)
    return jnp.sum(tiles.astype(jnp.float32), axis=0)


def joined_along(tiles, dim):
    shape = list(tiles.shape[1:])
    shape[dim] *= tiles.shape[0]
    return jnp.moveaxis(tiles, 0, dim).reshape(shape)


def copy_for_each(shard, axis):
    copies = jnp.broadcast_to(shard, (lax.axis_size(axis), *shard.shape))
    return lax.all_to_all(copies, axis, split_axis=0, concat_axis=0, tiled=True)


def gathered_copies(shard, axis, dim):
    return joined_along(copy_for_each(shard, axis), dim)


def ancestry(parent_row):
    node_count = parent_row.shape[0]
    position = jnp.arange(node_count, dtype=jnp.int32)
    reached = (parent_row[:, None] == position[None, :]).astype(jnp.float32)
    reached = reached + jnp.eye(node_count, dtype=jnp.float32)
    for doubling in range((node_count - 1).bit_length()):
        reached = jnp.minimum(jnp.dot(reached, reached, preferred_element_type=jnp.float32), 1.0)
    return reached > 0.5


def quarter_to_whole(received):
    return lax.all_gather(received, "tp", axis=2, tiled=True)


def attend_local(
    queries, cached_key_rows, cached_value_rows, tree_key_rows, tree_value_rows, lengths, parents
):
    request_count = lengths.shape[0]
    node_count = parents.shape[1]
    slot_length = cached_key_rows.shape[1]
    kv_local = cached_key_rows.shape[2] // HEAD_SIZE
    query_group_count = queries.shape[1] // (kv_local * HEAD_SIZE)
    scaled = 1.0 / math.sqrt(HEAD_SIZE)
    tree_query_block = queries.reshape(
        request_count, node_count, kv_local, query_group_count, HEAD_SIZE
    )
    joined_key_block = cached_key_rows.reshape(request_count, slot_length, kv_local, HEAD_SIZE)
    joined_value_block = cached_value_rows.reshape(request_count, slot_length, kv_local, HEAD_SIZE)
    tree_key_block = tree_key_rows.reshape(request_count, node_count, kv_local, HEAD_SIZE)
    tree_value_block = tree_value_rows.reshape(request_count, node_count, kv_local, HEAD_SIZE)
    cache_scores = (
        jnp.einsum(
            "rnkgd,rpkd->rkgnp",
            tree_query_block,
            joined_key_block,
            preferred_element_type=jnp.float32,
        )
        * scaled
    )
    tree_scores = (
        jnp.einsum(
            "rnkgd,rmkd->rkgnm",
            tree_query_block,
            tree_key_block,
            preferred_element_type=jnp.float32,
        )
        * scaled
    )
    visible = jnp.arange(slot_length, dtype=jnp.int32)[None, :] < lengths[:, None]
    cache_scores = jnp.where(visible[:, None, None, None, :], cache_scores, -1e30)
    related = jax.vmap(ancestry)(parents)
    tree_scores = jnp.where(related[:, None, None], tree_scores, -1e30)
    highest = jnp.maximum(jnp.max(cache_scores, axis=-1), jnp.max(tree_scores, axis=-1))[..., None]
    cache_raised = jnp.exp(cache_scores - highest)
    tree_raised = jnp.exp(tree_scores - highest)
    denominator = jnp.sum(cache_raised, axis=-1, keepdims=True) + jnp.sum(
        tree_raised, axis=-1, keepdims=True
    )
    cache_weights = (cache_raised / denominator).astype(jnp.bfloat16)
    tree_weights = (tree_raised / denominator).astype(jnp.bfloat16)
    output = jnp.einsum(
        "rkgnp,rpkd->rnkgd", cache_weights, joined_value_block, preferred_element_type=jnp.float32
    )
    output = output + jnp.einsum(
        "rkgnm,rmkd->rnkgd", tree_weights, tree_value_block, preferred_element_type=jnp.float32
    )
    return output.reshape(request_count * node_count, -1).astype(jnp.bfloat16)


def on_device(
    hidden,
    routes,
    routing_weights,
    w_gate,
    w_up,
    w_down,
    norm_gain,
    key_projection_weight,
    value_projection_weight,
    queries,
    cached_key_rows,
    cached_value_rows,
    lengths,
    parents,
):
    token_count = hidden.shape[0]
    top_count = routes.shape[1]
    local_experts = w_gate.shape[0]
    expert_count = lax.axis_size("dp") * local_experts
    capacity = min(token_count, 2 * token_count * top_count // expert_count)
    column_count = hidden.shape[1]
    weights = routing_weights / jnp.sum(routing_weights, axis=1, keepdims=True)
    expert_ids = jnp.arange(expert_count, dtype=jnp.int32)
    chosen = routes[:, :, None] == expert_ids[None, None, :]
    member = jnp.any(chosen, axis=1)
    portion = jnp.sum(jnp.where(chosen, weights[:, :, None], 0.0), axis=1)
    earlier = jnp.tril(jnp.ones((token_count, token_count), jnp.bfloat16), -1)
    rank = jnp.dot(earlier, member.astype(jnp.bfloat16), preferred_element_type=jnp.float32)
    slots = jnp.arange(capacity, dtype=jnp.float32)
    placed = member.T[:, None, :] & (rank.T[:, None, :] == slots[None, :, None])
    placed = placed.reshape(expert_count * capacity, token_count)
    outgoing = jnp.dot(
        placed.astype(jnp.bfloat16), hidden, preferred_element_type=jnp.float32
    ).astype(jnp.bfloat16)
    outgoing = outgoing.reshape(expert_count, capacity, column_count)
    received = quarter_to_whole(
        lax.all_to_all(outgoing, "dp", split_axis=0, concat_axis=0, tiled=True)
    )
    slot_count = received.shape[1]
    grouped = received.reshape(-1, local_experts, slot_count, received.shape[2])
    gate_act = jnp.einsum("secd,edf->secf", grouped, w_gate, preferred_element_type=jnp.float32)
    upward = jnp.einsum("secd,edf->secf", grouped, w_up, preferred_element_type=jnp.float32)
    active = (jax.nn.silu(gate_act) * upward).astype(jnp.bfloat16)
    partial_value = jnp.einsum("secf,efd->secd", active, w_down, preferred_element_type=jnp.float32)
    partial_value = partial_value.reshape(received.shape[0], slot_count, partial_value.shape[3])
    summed = sent_and_summed(partial_value.astype(jnp.bfloat16), "tp", 2)
    back = lax.all_to_all(
        summed.astype(jnp.bfloat16), "dp", split_axis=0, concat_axis=0, tiled=True
    )
    flat_back = back.reshape(expert_count * capacity, back.shape[2])
    spread = jnp.broadcast_to(portion.T[:, None, :], (expert_count, capacity, token_count))
    spread = jnp.where(placed, spread.reshape(expert_count * capacity, token_count), 0.0)
    upper = spread.astype(jnp.bfloat16)
    lower = (spread - upper.astype(jnp.float32)).astype(jnp.bfloat16)
    both = jnp.concatenate([upper, lower], axis=1)
    mixed = lax.dot_general(
        both, flat_back, (((0,), (0,)), ((), ())), preferred_element_type=jnp.float32
    )
    expert_mix = mixed[:token_count] + mixed[token_count:]
    own_out = (hidden.astype(jnp.float32) + expert_mix).astype(jnp.bfloat16)
    full_out = gathered_copies(own_out, "tp", 1)
    widened = full_out.astype(jnp.float32)
    scaling = lax.rsqrt(jnp.mean(widened * widened, axis=1, keepdims=True) + 1e-06)
    normed = (widened * scaling * norm_gain).astype(jnp.bfloat16)
    tree_key_rows = jnp.dot(
        normed, key_projection_weight, preferred_element_type=jnp.float32
    ).astype(jnp.bfloat16)
    tree_value_rows = jnp.dot(
        normed, value_projection_weight, preferred_element_type=jnp.float32
    ).astype(jnp.bfloat16)
    attended = attend_local(
        queries,
        cached_key_rows,
        cached_value_rows,
        tree_key_rows,
        tree_value_rows,
        lengths,
        parents,
    )
    return (own_out, tree_key_rows, tree_value_rows, attended)


def solution(mesh):
    return jax.shard_map(
        on_device,
        mesh=mesh,
        in_specs=(
            P("dp", "tp"),
            P("dp", None),
            P("dp", None),
            P("dp", None, "tp"),
            P("dp", None, "tp"),
            P("dp", "tp", None),
            P(),
            P(None, "tp"),
            P(None, "tp"),
            P("dp", "tp"),
            P("dp", None, "tp"),
            P("dp", None, "tp"),
            P("dp"),
            P("dp", None),
        ),
        out_specs=(P("dp", "tp"), P("dp", "tp"), P("dp", "tp"), P("dp", "tp")),
        check_vma=False,
    )
```

```python
import math

import jax
import jax.numpy as jnp
from jax import lax
from jax.experimental import pallas as pl
from jax.sharding import PartitionSpec as P

HEAD_SIZE = 128
CHUNKS = 1


def shifted(value, step):
    size = lax.axis_size("tp")
    return lax.ppermute(value, "tp", [(i, (i + step) % size) for i in range(size)])


def gathered_ring(rows):
    half = rows.shape[0] // 2
    before = shifted(rows, 1)
    after = shifted(rows, -1)
    opposite = jnp.concatenate([shifted(before[:half], 1), shifted(after[half:], -1)], axis=0)
    return rows, before, after, opposite


def around(value, dim, size):
    index = lax.axis_index("tp")
    count = lax.axis_size("tp")
    return [
        lax.dynamic_slice_in_dim(value, ((index + step) % count) * size, size, dim)
        for step in (0, count - 1, 1, 2)
    ]


def sent_around(blocks):
    to_before, to_after, to_opposite = blocks
    return shifted(to_after, 1), shifted(to_before, -1), shifted(to_opposite, 2)


def summed_products(blocks, weights):
    total = jnp.dot(blocks[0], weights[0], preferred_element_type=jnp.float32)
    for block, weight in zip(blocks[1:], weights[1:]):
        total = total + jnp.dot(block, weight, preferred_element_type=jnp.float32)
    return total


def joined_along(tiles, dim):
    shape = list(tiles.shape[1:])
    shape[dim] *= tiles.shape[0]
    return jnp.moveaxis(tiles, 0, dim).reshape(shape)


def copy_for_each(shard, axis):
    copies = jnp.broadcast_to(shard, (lax.axis_size(axis), *shard.shape))
    return lax.all_to_all(copies, axis, split_axis=0, concat_axis=0, tiled=True)


def gathered_copies(shard, axis, dim):
    return joined_along(copy_for_each(shard, axis), dim)


def ancestry_kernel(parents_ref, related_ref):
    node_count = parents_ref.shape[0]
    column = lax.broadcasted_iota(jnp.int32, (node_count, node_count), 1)
    row = lax.broadcasted_iota(jnp.int32, (node_count, node_count), 0)
    reached = jnp.where((parents_ref[...] == column) | (row == column), 1.0, 0.0)
    for doubling in range((node_count - 1).bit_length()):
        product = jnp.dot(reached, reached, preferred_element_type=jnp.float32)
        reached = jnp.minimum(product, 1.0)
    related_ref[...] = reached


def ancestry(parents):
    node_count = parents.shape[1]
    return pl.pallas_call(
        ancestry_kernel,
        out_shape=jax.ShapeDtypeStruct((node_count, node_count), jnp.float32),
        cost_estimate=pl.CostEstimate(flops=23070000000, bytes_accessed=8192, transcendentals=0),
    )(parents.reshape(node_count, 1))


def attend_local(
    queries, cached_key_rows, cached_value_rows, tree_key_rows, tree_value_rows, lengths, related
):
    request_count = lengths.shape[0]
    node_count = related.shape[0]
    slot_length = cached_key_rows.shape[1]
    kv_local = cached_key_rows.shape[2] // HEAD_SIZE
    query_group_count = queries.shape[1] // (kv_local * HEAD_SIZE)
    scaled = 1.0 / math.sqrt(HEAD_SIZE)
    tree_query_block = queries.reshape(
        request_count, node_count, kv_local, query_group_count, HEAD_SIZE
    )
    joined_key_block = cached_key_rows.reshape(request_count, slot_length, kv_local, HEAD_SIZE)
    joined_value_block = cached_value_rows.reshape(request_count, slot_length, kv_local, HEAD_SIZE)
    tree_key_block = tree_key_rows.reshape(request_count, node_count, kv_local, HEAD_SIZE)
    tree_value_block = tree_value_rows.reshape(request_count, node_count, kv_local, HEAD_SIZE)
    cache_scores = (
        jnp.einsum(
            "rnkgd,rpkd->rkgnp",
            tree_query_block,
            joined_key_block,
            preferred_element_type=jnp.float32,
        )
        * scaled
    )
    tree_scores = (
        jnp.einsum(
            "rnkgd,rmkd->rkgnm",
            tree_query_block,
            tree_key_block,
            preferred_element_type=jnp.float32,
        )
        * scaled
    )
    visible = jnp.arange(slot_length, dtype=jnp.int32)[None, :] < lengths[:, None]
    cache_scores = jnp.where(visible[:, None, None, None, :], cache_scores, -1e30)
    tree_scores = jnp.where(related[None, None, None] > 0.5, tree_scores, -1e30)
    highest = jnp.maximum(jnp.max(cache_scores, axis=-1), jnp.max(tree_scores, axis=-1))[..., None]
    cache_raised = jnp.exp(cache_scores - highest)
    tree_raised = jnp.exp(tree_scores - highest)
    denominator = jnp.sum(cache_raised, axis=-1, keepdims=True) + jnp.sum(
        tree_raised, axis=-1, keepdims=True
    )
    cache_weights = (cache_raised / denominator).astype(jnp.bfloat16)
    tree_weights = (tree_raised / denominator).astype(jnp.bfloat16)
    output = jnp.einsum(
        "rkgnp,rpkd->rnkgd", cache_weights, joined_value_block, preferred_element_type=jnp.float32
    )
    output = output + jnp.einsum(
        "rkgnm,rmkd->rnkgd", tree_weights, tree_value_block, preferred_element_type=jnp.float32
    )
    return output.reshape(request_count * node_count, -1).astype(jnp.bfloat16)


def on_device(
    hidden,
    routes,
    routing_weights,
    w_gate,
    w_up,
    w_down,
    norm_gain,
    key_projection_weight,
    value_projection_weight,
    queries,
    cached_key_rows,
    cached_value_rows,
    lengths,
    parents,
):
    token_count = hidden.shape[0]
    top_count = routes.shape[1]
    expert_count = lax.axis_size("dp")
    capacity = min(token_count, 2 * token_count * top_count // expert_count)
    column_count = hidden.shape[1]
    down_own, *down_sent = around(w_down[0], 1, column_count)
    routes, routing_weights, down_sent = lax.optimization_barrier((routes, routing_weights, down_sent))
    weights = routing_weights / jnp.sum(routing_weights, axis=1, keepdims=True)
    expert_ids = jnp.arange(expert_count, dtype=jnp.int32)
    chosen = routes[:, :, None] == expert_ids[None, None, :]
    member = jnp.any(chosen, axis=1)
    portion = jnp.sum(jnp.where(chosen, weights[:, :, None], 0.0), axis=1)
    earlier = jnp.tril(jnp.ones((token_count, token_count), jnp.bfloat16), -1)
    rank = jnp.dot(earlier, member.astype(jnp.bfloat16), preferred_element_type=jnp.float32)
    slots = jnp.arange(capacity, dtype=jnp.float32)
    placed = member.T[:, None, :] & (rank.T[:, None, :] == slots[None, :, None])
    placed = placed.reshape(expert_count * capacity, token_count)
    outgoing = jnp.dot(
        placed.astype(jnp.bfloat16), hidden, preferred_element_type=jnp.float32
    ).astype(jnp.bfloat16)
    outgoing = outgoing.reshape(expert_count, capacity, column_count)
    down_received = sent_around(down_sent)
    down_received, parents = lax.optimization_barrier((down_received, parents))
    related = ancestry(parents)
    down_blocks = [down_own, *down_received]
    hidden_units = w_gate.shape[2]
    both_weights = [
        jnp.concatenate(pair, axis=1)
        for pair in zip(around(w_gate[0], 0, column_count), around(w_up[0], 0, column_count))
    ]
    received = lax.all_to_all(outgoing, "dp", split_axis=0, concat_axis=0, tiled=True)
    received, down_blocks, both_weights, related = lax.optimization_barrier(
        (received, down_blocks, both_weights, related)
    )
    chunk = capacity // CHUNKS
    returned = []
    for part in range(CHUNKS):
        rows = received[:, part * chunk : (part + 1) * chunk].reshape(expert_count * chunk, column_count)
        products = summed_products(gathered_ring(rows), both_weights)
        gate_act, upward = products[:, :hidden_units], products[:, hidden_units:]
        active = (jax.nn.silu(gate_act) * upward).astype(jnp.bfloat16)
        made = summed_products(gathered_ring(active), down_blocks).astype(jnp.bfloat16)
        returned.append(
            lax.all_to_all(
                made.reshape(expert_count, chunk, column_count), "dp", split_axis=0, concat_axis=0, tiled=True
            )
        )
    flat_back = jnp.concatenate(returned, axis=1).reshape(expert_count * capacity, column_count)
    spread = jnp.broadcast_to(portion.T[:, None, :], (expert_count, capacity, token_count))
    spread = jnp.where(placed, spread.reshape(expert_count * capacity, token_count), 0.0)
    upper = spread.astype(jnp.bfloat16)
    lower = (spread - upper.astype(jnp.float32)).astype(jnp.bfloat16)
    both = jnp.concatenate([upper, lower], axis=1)
    mixed = lax.dot_general(
        both, flat_back, (((0,), (0,)), ((), ())), preferred_element_type=jnp.float32
    )
    expert_mix = mixed[:token_count] + mixed[token_count:]
    own_out = (hidden.astype(jnp.float32) + expert_mix).astype(jnp.bfloat16)
    full_out = gathered_copies(own_out, "tp", 1)
    widened = full_out.astype(jnp.float32)
    scaling = lax.rsqrt(jnp.mean(widened * widened, axis=1, keepdims=True) + 1e-06)
    normed = (widened * scaling * norm_gain).astype(jnp.bfloat16)
    tree_key_rows = jnp.dot(
        normed, key_projection_weight, preferred_element_type=jnp.float32
    ).astype(jnp.bfloat16)
    tree_value_rows = jnp.dot(
        normed, value_projection_weight, preferred_element_type=jnp.float32
    ).astype(jnp.bfloat16)
    attended = attend_local(
        queries,
        cached_key_rows,
        cached_value_rows,
        tree_key_rows,
        tree_value_rows,
        lengths,
        related,
    )
    return (own_out, tree_key_rows, tree_value_rows, attended)


def solution(mesh):
    return jax.shard_map(
        on_device,
        mesh=mesh,
        in_specs=(
            P("dp", "tp"),
            P("dp", None),
            P("dp", None),
            P("dp", None, "tp"),
            P("dp", None, "tp"),
            P("dp", "tp", None),
            P(),
            P(None, "tp"),
            P(None, "tp"),
            P("dp", "tp"),
            P("dp", None, "tp"),
            P("dp", None, "tp"),
            P("dp"),
            P("dp", None),
        ),
        out_specs=(P("dp", "tp"), P("dp", "tp"), P("dp", "tp"), P("dp", "tp")),
        check_vma=False,
    )
```

```python
import math

import jax
import jax.numpy as jnp
from jax import lax
from jax.experimental import pallas as pl
from jax.sharding import PartitionSpec as P

HEAD_SIZE = 128
CHUNKS = 1


def shifted(value, step):
    size = lax.axis_size("tp")
    return lax.ppermute(value, "tp", [(i, (i + step) % size) for i in range(size)])


def gathered_ring(rows):
    half = rows.shape[0] // 2
    upper, lower = rows[:half], rows[half:]
    before_upper, after_lower = shifted(upper, 1), shifted(lower, -1)
    before_lower, after_upper = shifted(lower, 1), shifted(upper, -1)
    opposite = jnp.concatenate([shifted(before_upper, 1), shifted(after_lower, -1)], axis=0)
    before = jnp.concatenate([before_upper, before_lower], axis=0)
    after = jnp.concatenate([after_upper, after_lower], axis=0)
    return rows, before, after, opposite


def around(value, dim, size):
    index = lax.axis_index("tp")
    count = lax.axis_size("tp")
    return [
        lax.dynamic_slice_in_dim(value, ((index + step) % count) * size, size, dim)
        for step in (0, count - 1, 1, 2)
    ]


def sent_around(blocks):
    to_before, to_after, to_opposite = blocks
    return shifted(to_after, 1), shifted(to_before, -1), shifted(to_opposite, 2)


def summed_products(blocks, weights):
    total = jnp.dot(blocks[0], weights[0], preferred_element_type=jnp.float32)
    for block, weight in zip(blocks[1:], weights[1:]):
        total = total + jnp.dot(block, weight, preferred_element_type=jnp.float32)
    return total


def joined_along(tiles, dim):
    shape = list(tiles.shape[1:])
    shape[dim] *= tiles.shape[0]
    return jnp.moveaxis(tiles, 0, dim).reshape(shape)


def copy_for_each(shard, axis):
    copies = jnp.broadcast_to(shard, (lax.axis_size(axis), *shard.shape))
    return lax.all_to_all(copies, axis, split_axis=0, concat_axis=0, tiled=True)


def gathered_copies(shard, axis, dim):
    return joined_along(copy_for_each(shard, axis), dim)


def ancestry_kernel(parents_ref, related_ref):
    node_count = parents_ref.shape[0]
    column = lax.broadcasted_iota(jnp.int32, (node_count, node_count), 1)
    row = lax.broadcasted_iota(jnp.int32, (node_count, node_count), 0)
    reached = jnp.where((parents_ref[...] == column) | (row == column), 1.0, 0.0)
    for doubling in range((node_count - 1).bit_length()):
        product = jnp.dot(reached, reached, preferred_element_type=jnp.float32)
        reached = jnp.minimum(product, 1.0)
    related_ref[...] = reached


def ancestry(parents):
    node_count = parents.shape[1]
    return pl.pallas_call(
        ancestry_kernel,
        out_shape=jax.ShapeDtypeStruct((node_count, node_count), jnp.float32),
        cost_estimate=pl.CostEstimate(flops=23070000000, bytes_accessed=8192, transcendentals=0),
    )(parents.reshape(node_count, 1))


def attend_local(
    queries, cached_key_rows, cached_value_rows, tree_key_rows, tree_value_rows, lengths, related
):
    request_count = lengths.shape[0]
    node_count = related.shape[0]
    slot_length = cached_key_rows.shape[1]
    kv_local = cached_key_rows.shape[2] // HEAD_SIZE
    query_group_count = queries.shape[1] // (kv_local * HEAD_SIZE)
    scaled = 1.0 / math.sqrt(HEAD_SIZE)
    tree_query_block = queries.reshape(
        request_count, node_count, kv_local, query_group_count, HEAD_SIZE
    )
    joined_key_block = cached_key_rows.reshape(request_count, slot_length, kv_local, HEAD_SIZE)
    joined_value_block = cached_value_rows.reshape(request_count, slot_length, kv_local, HEAD_SIZE)
    tree_key_block = tree_key_rows.reshape(request_count, node_count, kv_local, HEAD_SIZE)
    tree_value_block = tree_value_rows.reshape(request_count, node_count, kv_local, HEAD_SIZE)
    cache_scores = (
        jnp.einsum(
            "rnkgd,rpkd->rkgnp",
            tree_query_block,
            joined_key_block,
            preferred_element_type=jnp.float32,
        )
        * scaled
    )
    tree_scores = (
        jnp.einsum(
            "rnkgd,rmkd->rkgnm",
            tree_query_block,
            tree_key_block,
            preferred_element_type=jnp.float32,
        )
        * scaled
    )
    visible = jnp.arange(slot_length, dtype=jnp.int32)[None, :] < lengths[:, None]
    cache_scores = jnp.where(visible[:, None, None, None, :], cache_scores, -1e30)
    tree_scores = jnp.where(related[None, None, None] > 0.5, tree_scores, -1e30)
    highest = jnp.maximum(jnp.max(cache_scores, axis=-1), jnp.max(tree_scores, axis=-1))[..., None]
    cache_raised = jnp.exp(cache_scores - highest)
    tree_raised = jnp.exp(tree_scores - highest)
    denominator = jnp.sum(cache_raised, axis=-1, keepdims=True) + jnp.sum(
        tree_raised, axis=-1, keepdims=True
    )
    cache_weights = (cache_raised / denominator).astype(jnp.bfloat16)
    tree_weights = (tree_raised / denominator).astype(jnp.bfloat16)
    output = jnp.einsum(
        "rkgnp,rpkd->rnkgd", cache_weights, joined_value_block, preferred_element_type=jnp.float32
    )
    output = output + jnp.einsum(
        "rkgnm,rmkd->rnkgd", tree_weights, tree_value_block, preferred_element_type=jnp.float32
    )
    return output.reshape(request_count * node_count, -1).astype(jnp.bfloat16)


def on_device(
    hidden,
    routes,
    routing_weights,
    w_gate,
    w_up,
    w_down,
    norm_gain,
    key_projection_weight,
    value_projection_weight,
    queries,
    cached_key_rows,
    cached_value_rows,
    lengths,
    parents,
):
    token_count = hidden.shape[0]
    top_count = routes.shape[1]
    expert_count = lax.axis_size("dp")
    capacity = min(token_count, 2 * token_count * top_count // expert_count)
    column_count = hidden.shape[1]
    down_own, *down_sent = around(w_down[0], 1, column_count)
    routes, routing_weights, down_sent = lax.optimization_barrier((routes, routing_weights, down_sent))
    weights = routing_weights / jnp.sum(routing_weights, axis=1, keepdims=True)
    expert_ids = jnp.arange(expert_count, dtype=jnp.int32)
    chosen = routes[:, :, None] == expert_ids[None, None, :]
    member = jnp.any(chosen, axis=1)
    portion = jnp.sum(jnp.where(chosen, weights[:, :, None], 0.0), axis=1)
    earlier = jnp.tril(jnp.ones((token_count, token_count), jnp.bfloat16), -1)
    rank = jnp.dot(earlier, member.astype(jnp.bfloat16), preferred_element_type=jnp.float32)
    slots = jnp.arange(capacity, dtype=jnp.float32)
    placed = member.T[:, None, :] & (rank.T[:, None, :] == slots[None, :, None])
    placed = placed.reshape(expert_count * capacity, token_count)
    outgoing = jnp.dot(
        placed.astype(jnp.bfloat16), hidden, preferred_element_type=jnp.float32
    ).astype(jnp.bfloat16)
    outgoing = outgoing.reshape(expert_count, capacity, column_count)
    down_received = sent_around(down_sent)
    down_whole = jnp.concatenate([down_own, *down_received], axis=0)
    down_whole, parents = lax.optimization_barrier((down_whole, parents))
    related = ancestry(parents)
    hidden_units = w_gate.shape[2]
    both_weights = [
        jnp.concatenate(pair, axis=1)
        for pair in zip(around(w_gate[0], 0, column_count), around(w_up[0], 0, column_count))
    ]
    received = lax.all_to_all(outgoing, "dp", split_axis=0, concat_axis=0, tiled=True)
    received, down_whole, both_weights, related = lax.optimization_barrier(
        (received, down_whole, both_weights, related)
    )
    down_blocks = jnp.split(down_whole, lax.axis_size("tp"))
    chunk = capacity // CHUNKS
    returned = []
    for part in range(CHUNKS):
        rows = received[:, part * chunk : (part + 1) * chunk].reshape(expert_count * chunk, column_count)
        products = summed_products(gathered_ring(rows), both_weights)
        gate_act, upward = products[:, :hidden_units], products[:, hidden_units:]
        active = (jax.nn.silu(gate_act) * upward).astype(jnp.bfloat16)
        made = summed_products(gathered_ring(active), down_blocks).astype(jnp.bfloat16)
        returned.append(
            lax.all_to_all(
                made.reshape(expert_count, chunk, column_count), "dp", split_axis=0, concat_axis=0, tiled=True
            )
        )
    flat_back = jnp.concatenate(returned, axis=1).reshape(expert_count * capacity, column_count)
    spread = jnp.broadcast_to(portion.T[:, None, :], (expert_count, capacity, token_count))
    spread = jnp.where(placed, spread.reshape(expert_count * capacity, token_count), 0.0)
    upper = spread.astype(jnp.bfloat16)
    lower = (spread - upper.astype(jnp.float32)).astype(jnp.bfloat16)
    both = jnp.concatenate([upper, lower], axis=1)
    mixed = lax.dot_general(
        both, flat_back, (((0,), (0,)), ((), ())), preferred_element_type=jnp.float32
    )
    expert_mix = mixed[:token_count] + mixed[token_count:]
    own_out = (hidden.astype(jnp.float32) + expert_mix).astype(jnp.bfloat16)
    full_out = gathered_copies(own_out, "tp", 1)
    widened = full_out.astype(jnp.float32)
    scaling = lax.rsqrt(jnp.mean(widened * widened, axis=1, keepdims=True) + 1e-06)
    normed = (widened * scaling * norm_gain).astype(jnp.bfloat16)
    tree_key_rows = jnp.dot(
        normed, key_projection_weight, preferred_element_type=jnp.float32
    ).astype(jnp.bfloat16)
    tree_value_rows = jnp.dot(
        normed, value_projection_weight, preferred_element_type=jnp.float32
    ).astype(jnp.bfloat16)
    attended = attend_local(
        queries,
        cached_key_rows,
        cached_value_rows,
        tree_key_rows,
        tree_value_rows,
        lengths,
        related,
    )
    return (own_out, tree_key_rows, tree_value_rows, attended)


def solution(mesh):
    return jax.shard_map(
        on_device,
        mesh=mesh,
        in_specs=(
            P("dp", "tp"),
            P("dp", None),
            P("dp", None),
            P("dp", None, "tp"),
            P("dp", None, "tp"),
            P("dp", "tp", None),
            P(),
            P(None, "tp"),
            P(None, "tp"),
            P("dp", "tp"),
            P("dp", None, "tp"),
            P("dp", None, "tp"),
            P("dp"),
            P("dp", None),
        ),
        out_specs=(P("dp", "tp"), P("dp", "tp"), P("dp", "tp"), P("dp", "tp")),
        check_vma=False,
    )
```

```python
import math

import jax
import jax.numpy as jnp
from jax import lax
from jax.experimental import pallas as pl
from jax.experimental.pallas import tpu as pltpu
from jax.sharding import PartitionSpec as P

HEAD_SIZE = 128
EXPERT_COLUMNS = 64
CHUNKS = 1


def shifted(value, step):
    size = lax.axis_size("tp")
    return lax.ppermute(value, "tp", [(i, (i + step) % size) for i in range(size)])


def gathered_ring(rows):
    half = rows.shape[0] // 2
    upper, lower = rows[:half], rows[half:]
    before_upper, after_lower = shifted(upper, 1), shifted(lower, -1)
    before_lower, after_upper = shifted(lower, 1), shifted(upper, -1)
    opposite = jnp.concatenate([shifted(before_upper, 1), shifted(after_lower, -1)], axis=0)
    before = jnp.concatenate([before_upper, before_lower], axis=0)
    after = jnp.concatenate([after_upper, after_lower], axis=0)
    return rows, before, after, opposite


def routed_kernel(routes_ref, scores_ref, hidden_ref, sent_ref, combine_ref):
    top_count, token_count = routes_ref.shape
    slot_total = sent_ref.shape[0]
    capacity = slot_total // EXPERT_COLUMNS
    routes = routes_ref[...]
    weights = scores_ref[...] / jnp.sum(scores_ref[...], axis=0, keepdims=True)
    expert = lax.broadcasted_iota(jnp.int32, (EXPERT_COLUMNS, token_count), 0)
    member = jnp.zeros((EXPERT_COLUMNS, token_count), jnp.float32)
    portion = jnp.zeros((EXPERT_COLUMNS, token_count), jnp.float32)
    for k in range(top_count):
        named = routes[k : k + 1, :] == expert
        member = jnp.where(named, 1.0, member)
        portion = jnp.where(named, weights[k : k + 1, :], portion)
    earlier = lax.broadcasted_iota(jnp.int32, (token_count, token_count), 0) < lax.broadcasted_iota(
        jnp.int32, (token_count, token_count), 1
    )
    earlier = jnp.where(earlier, 1.0, 0.0).astype(jnp.bfloat16)
    rank = jnp.dot(member.astype(jnp.bfloat16), earlier, preferred_element_type=jnp.float32)
    key = jnp.where(member > 0.5, rank, -1.0)
    upper = portion.astype(jnp.bfloat16).astype(jnp.float32)
    lower = portion - upper
    slot = lax.broadcasted_iota(jnp.int32, (slot_total, EXPERT_COLUMNS), 0)
    first = lax.broadcasted_iota(jnp.int32, (slot_total, EXPERT_COLUMNS), 1) * capacity
    of_expert = jnp.where((slot >= first) & (slot < first + capacity), 1.0, 0.0).astype(jnp.bfloat16)
    table = jnp.concatenate([key, upper, lower], axis=1).astype(jnp.bfloat16)
    spread = jnp.dot(of_expert, table, preferred_element_type=jnp.float32)
    place = lax.rem(lax.broadcasted_iota(jnp.int32, (slot_total, token_count), 0), capacity)
    chosen = jnp.where(spread[:, :token_count] == place.astype(jnp.float32), 1.0, 0.0)
    sent_ref[...] = jnp.dot(
        chosen.astype(jnp.bfloat16), hidden_ref[...], preferred_element_type=jnp.float32
    ).astype(sent_ref.dtype)
    both = jnp.concatenate([chosen, chosen], axis=1)
    combine_ref[...] = (both * spread[:, token_count:]).astype(combine_ref.dtype)


def routed_rows(routes, scores, hidden, capacity):
    slot_total = EXPERT_COLUMNS * capacity
    token_count, width = hidden.shape
    return pl.pallas_call(
        routed_kernel,
        out_shape=[
            jax.ShapeDtypeStruct((slot_total, width), hidden.dtype),
            jax.ShapeDtypeStruct((slot_total, 2 * token_count), jnp.bfloat16),
        ],
        compiler_params=pltpu.CompilerParams(vmem_limit_bytes=12 << 20),
        cost_estimate=pl.CostEstimate(flops=1 << 26, bytes_accessed=3 * slot_total * width, transcendentals=0),
    )(routes.T, scores.T, hidden)


def around(value, dim, size):
    index = lax.axis_index("tp")
    count = lax.axis_size("tp")
    return [
        lax.dynamic_slice_in_dim(value, ((index + step) % count) * size, size, dim)
        for step in (0, count - 1, 1, 2)
    ]


def sent_around(blocks):
    to_before, to_after, to_opposite = blocks
    return shifted(to_after, 1), shifted(to_before, -1), shifted(to_opposite, 2)


def summed_products(blocks, weights):
    total = jnp.dot(blocks[0], weights[0], preferred_element_type=jnp.float32)
    for block, weight in zip(blocks[1:], weights[1:]):
        total = total + jnp.dot(block, weight, preferred_element_type=jnp.float32)
    return total


def joined_along(tiles, dim):
    shape = list(tiles.shape[1:])
    shape[dim] *= tiles.shape[0]
    return jnp.moveaxis(tiles, 0, dim).reshape(shape)


def copy_for_each(shard, axis):
    copies = jnp.broadcast_to(shard, (lax.axis_size(axis), *shard.shape))
    return lax.all_to_all(copies, axis, split_axis=0, concat_axis=0, tiled=True)


def gathered_copies(shard, axis, dim):
    return joined_along(copy_for_each(shard, axis), dim)


def parent_kernel(parents_ref, reached_ref):
    node_count = parents_ref.shape[1]
    row = lax.broadcasted_iota(jnp.int32, (node_count, node_count), 0)
    column = lax.broadcasted_iota(jnp.int32, (node_count, node_count), 1)
    reached_ref[...] = jnp.where((parents_ref[...] == row) | (row == column), 1.0, 0.0)


def own_and_parents(parents):
    node_count = parents.shape[1]
    return pl.pallas_call(
        parent_kernel,
        out_shape=jax.ShapeDtypeStruct((node_count, node_count), jnp.float32),
        cost_estimate=pl.CostEstimate(flops=23070000000, bytes_accessed=8192, transcendentals=0),
    )(parents)


def ancestry(reached):
    for doubling in range((reached.shape[0] - 1).bit_length()):
        reached = jnp.minimum(jnp.dot(reached, reached, preferred_element_type=jnp.float32), 1.0)
    return reached.T


def attend_local(
    queries, cached_key_rows, cached_value_rows, tree_key_rows, tree_value_rows, lengths, related
):
    request_count = lengths.shape[0]
    node_count = related.shape[0]
    slot_length = cached_key_rows.shape[1]
    kv_local = cached_key_rows.shape[2] // HEAD_SIZE
    query_group_count = queries.shape[1] // (kv_local * HEAD_SIZE)
    scaled = 1.0 / math.sqrt(HEAD_SIZE)
    tree_query_block = queries.reshape(
        request_count, node_count, kv_local, query_group_count, HEAD_SIZE
    )
    joined_key_block = cached_key_rows.reshape(request_count, slot_length, kv_local, HEAD_SIZE)
    joined_value_block = cached_value_rows.reshape(request_count, slot_length, kv_local, HEAD_SIZE)
    tree_key_block = tree_key_rows.reshape(request_count, node_count, kv_local, HEAD_SIZE)
    tree_value_block = tree_value_rows.reshape(request_count, node_count, kv_local, HEAD_SIZE)
    cache_scores = (
        jnp.einsum(
            "rnkgd,rpkd->rkgnp",
            tree_query_block,
            joined_key_block,
            preferred_element_type=jnp.float32,
        )
        * scaled
    )
    tree_scores = (
        jnp.einsum(
            "rnkgd,rmkd->rkgnm",
            tree_query_block,
            tree_key_block,
            preferred_element_type=jnp.float32,
        )
        * scaled
    )
    visible = jnp.arange(slot_length, dtype=jnp.int32)[None, :] < lengths[:, None]
    cache_scores = jnp.where(visible[:, None, None, None, :], cache_scores, -1e30)
    tree_scores = jnp.where(related[None, None, None] > 0.5, tree_scores, -1e30)
    highest = jnp.maximum(jnp.max(cache_scores, axis=-1), jnp.max(tree_scores, axis=-1))[..., None]
    cache_raised = jnp.exp(cache_scores - highest)
    tree_raised = jnp.exp(tree_scores - highest)
    denominator = jnp.sum(cache_raised, axis=-1, keepdims=True) + jnp.sum(
        tree_raised, axis=-1, keepdims=True
    )
    cache_weights = (cache_raised / denominator).astype(jnp.bfloat16)
    tree_weights = (tree_raised / denominator).astype(jnp.bfloat16)
    output = jnp.einsum(
        "rkgnp,rpkd->rnkgd", cache_weights, joined_value_block, preferred_element_type=jnp.float32
    )
    output = output + jnp.einsum(
        "rkgnm,rmkd->rnkgd", tree_weights, tree_value_block, preferred_element_type=jnp.float32
    )
    return output.reshape(request_count * node_count, -1).astype(jnp.bfloat16)


def on_device(
    hidden,
    routes,
    routing_weights,
    w_gate,
    w_up,
    w_down,
    norm_gain,
    key_projection_weight,
    value_projection_weight,
    queries,
    cached_key_rows,
    cached_value_rows,
    lengths,
    parents,
):
    token_count = hidden.shape[0]
    top_count = routes.shape[1]
    expert_count = lax.axis_size("dp")
    capacity = min(token_count, 2 * token_count * top_count // expert_count)
    column_count = hidden.shape[1]
    to_opposite = around(w_down[0], 1, column_count)[3]
    routes, routing_weights, to_opposite = lax.optimization_barrier((routes, routing_weights, to_opposite))
    outgoing, both = routed_rows(routes, routing_weights, hidden, capacity)
    outgoing = outgoing.reshape(expert_count, capacity, column_count)
    outgoing, w_down = lax.optimization_barrier((outgoing, w_down))
    down_own, to_before, to_after, _ = around(w_down[0], 1, column_count)
    before, after, opposite = sent_around((to_before, to_after, to_opposite))
    opposite, parents = lax.optimization_barrier((opposite, parents))
    reached = own_and_parents(parents)
    hidden_units = w_gate.shape[2]
    both_weights = [
        jnp.concatenate(pair, axis=1)
        for pair in zip(around(w_gate[0], 0, column_count), around(w_up[0], 0, column_count))
    ]
    received = lax.all_to_all(outgoing, "dp", split_axis=0, concat_axis=0, tiled=True)
    received, before, after, opposite, both_weights, reached = lax.optimization_barrier(
        (received, before, after, opposite, both_weights, reached)
    )
    down_whole = jnp.concatenate([down_own, before, after, opposite], axis=0)
    related = ancestry(reached)
    down_blocks = jnp.split(down_whole, lax.axis_size("tp"))
    chunk = capacity // CHUNKS
    returned = []
    for part in range(CHUNKS):
        rows = received[:, part * chunk : (part + 1) * chunk].reshape(expert_count * chunk, column_count)
        products = summed_products(gathered_ring(rows), both_weights)
        gate_act, upward = products[:, :hidden_units], products[:, hidden_units:]
        active = (jax.nn.silu(gate_act) * upward).astype(jnp.bfloat16)
        made = summed_products(gathered_ring(active), down_blocks).astype(jnp.bfloat16)
        returned.append(
            lax.all_to_all(
                made.reshape(expert_count, chunk, column_count), "dp", split_axis=0, concat_axis=0, tiled=True
            )
        )
    flat_back = jnp.concatenate(returned, axis=1).reshape(expert_count * capacity, column_count)
    mixed = lax.dot_general(
        both, flat_back, (((0,), (0,)), ((), ())), preferred_element_type=jnp.float32
    )
    expert_mix = mixed[:token_count] + mixed[token_count:]
    own_out = (hidden.astype(jnp.float32) + expert_mix).astype(jnp.bfloat16)
    full_out = gathered_copies(own_out, "tp", 1)
    widened = full_out.astype(jnp.float32)
    scaling = lax.rsqrt(jnp.mean(widened * widened, axis=1, keepdims=True) + 1e-06)
    normed = (widened * scaling * norm_gain).astype(jnp.bfloat16)
    tree_key_rows = jnp.dot(
        normed, key_projection_weight, preferred_element_type=jnp.float32
    ).astype(jnp.bfloat16)
    tree_value_rows = jnp.dot(
        normed, value_projection_weight, preferred_element_type=jnp.float32
    ).astype(jnp.bfloat16)
    attended = attend_local(
        queries,
        cached_key_rows,
        cached_value_rows,
        tree_key_rows,
        tree_value_rows,
        lengths,
        related,
    )
    return (own_out, tree_key_rows, tree_value_rows, attended)


def solution(mesh):
    return jax.shard_map(
        on_device,
        mesh=mesh,
        in_specs=(
            P("dp", "tp"),
            P("dp", None),
            P("dp", None),
            P("dp", None, "tp"),
            P("dp", None, "tp"),
            P("dp", "tp", None),
            P(),
            P(None, "tp"),
            P(None, "tp"),
            P("dp", "tp"),
            P("dp", None, "tp"),
            P("dp", None, "tp"),
            P("dp"),
            P("dp", None),
        ),
        out_specs=(P("dp", "tp"), P("dp", "tp"), P("dp", "tp"), P("dp", "tp")),
        check_vma=False,
    )
```

```python
import math

import jax
import jax.numpy as jnp
from jax import lax
from jax.experimental import pallas as pl
from jax.experimental.pallas import tpu as pltpu
from jax.sharding import PartitionSpec as P

HEAD_SIZE = 128
EXPERT_COLUMNS = 64
CHUNKS = 1


def shifted(value, step):
    size = lax.axis_size("tp")
    return lax.ppermute(value, "tp", [(i, (i + step) % size) for i in range(size)])


def gathered_ring(rows):
    half = rows.shape[0] // 2
    upper, lower = rows[:half], rows[half:]
    before_upper, after_lower = shifted(upper, 1), shifted(lower, -1)
    before_lower, after_upper = shifted(lower, 1), shifted(upper, -1)
    opposite = jnp.concatenate([shifted(before_upper, 1), shifted(after_lower, -1)], axis=0)
    before = jnp.concatenate([before_upper, before_lower], axis=0)
    after = jnp.concatenate([after_upper, after_lower], axis=0)
    return rows, before, after, opposite


def routed_kernel(routes_ref, scores_ref, hidden_ref, sent_ref, combine_ref):
    top_count, token_count = routes_ref.shape
    slot_total = sent_ref.shape[0]
    capacity = slot_total // EXPERT_COLUMNS
    routes = routes_ref[...]
    weights = scores_ref[...] / jnp.sum(scores_ref[...], axis=0, keepdims=True)
    expert = lax.broadcasted_iota(jnp.int32, (EXPERT_COLUMNS, token_count), 0)
    member = jnp.zeros((EXPERT_COLUMNS, token_count), jnp.float32)
    portion = jnp.zeros((EXPERT_COLUMNS, token_count), jnp.float32)
    for k in range(top_count):
        named = routes[k : k + 1, :] == expert
        member = jnp.where(named, 1.0, member)
        portion = jnp.where(named, weights[k : k + 1, :], portion)
    earlier = lax.broadcasted_iota(jnp.int32, (token_count, token_count), 0) < lax.broadcasted_iota(
        jnp.int32, (token_count, token_count), 1
    )
    earlier = jnp.where(earlier, 1.0, 0.0).astype(jnp.bfloat16)
    rank = jnp.dot(member.astype(jnp.bfloat16), earlier, preferred_element_type=jnp.float32)
    key = jnp.where(member > 0.5, rank, -1.0)
    upper = portion.astype(jnp.bfloat16).astype(jnp.float32)
    lower = portion - upper
    slot = lax.broadcasted_iota(jnp.int32, (slot_total, EXPERT_COLUMNS), 0)
    first = lax.broadcasted_iota(jnp.int32, (slot_total, EXPERT_COLUMNS), 1) * capacity
    of_expert = jnp.where((slot >= first) & (slot < first + capacity), 1.0, 0.0).astype(jnp.bfloat16)
    table = jnp.concatenate([key, upper, lower], axis=1).astype(jnp.bfloat16)
    spread = jnp.dot(of_expert, table, preferred_element_type=jnp.float32)
    place = lax.rem(lax.broadcasted_iota(jnp.int32, (slot_total, token_count), 0), capacity)
    chosen = jnp.where(spread[:, :token_count] == place.astype(jnp.float32), 1.0, 0.0)
    sent_ref[...] = jnp.dot(
        chosen.astype(jnp.bfloat16), hidden_ref[...], preferred_element_type=jnp.float32
    ).astype(sent_ref.dtype)
    both = jnp.concatenate([chosen, chosen], axis=1)
    combine_ref[...] = (both * spread[:, token_count:]).astype(combine_ref.dtype)


def routed_rows(routes, scores, hidden, capacity):
    slot_total = EXPERT_COLUMNS * capacity
    token_count, width = hidden.shape
    return pl.pallas_call(
        routed_kernel,
        out_shape=[
            jax.ShapeDtypeStruct((slot_total, width), hidden.dtype),
            jax.ShapeDtypeStruct((slot_total, 2 * token_count), jnp.bfloat16),
        ],
        compiler_params=pltpu.CompilerParams(vmem_limit_bytes=12 << 20),
        cost_estimate=pl.CostEstimate(flops=1 << 26, bytes_accessed=3 * slot_total * width, transcendentals=0),
    )(routes.T, scores.T, hidden)


def around(value, dim, size):
    index = lax.axis_index("tp")
    count = lax.axis_size("tp")
    return [
        lax.dynamic_slice_in_dim(value, ((index + step) % count) * size, size, dim)
        for step in (0, count - 1, 1, 2)
    ]


def sent_around(blocks):
    to_before, to_after, to_opposite = blocks
    return shifted(to_after, 1), shifted(to_before, -1), shifted(to_opposite, 2)


def summed_products(blocks, weights):
    total = jnp.dot(blocks[0], weights[0], preferred_element_type=jnp.float32)
    for block, weight in zip(blocks[1:], weights[1:]):
        total = total + jnp.dot(block, weight, preferred_element_type=jnp.float32)
    return total


def joined_along(tiles, dim):
    shape = list(tiles.shape[1:])
    shape[dim] *= tiles.shape[0]
    return jnp.moveaxis(tiles, 0, dim).reshape(shape)


def copy_for_each(shard, axis):
    copies = jnp.broadcast_to(shard, (lax.axis_size(axis), *shard.shape))
    return lax.all_to_all(copies, axis, split_axis=0, concat_axis=0, tiled=True)


def gathered_copies(shard, axis, dim):
    return joined_along(copy_for_each(shard, axis), dim)


def parent_kernel(parents_ref, reached_ref):
    node_count = parents_ref.shape[1]
    row = lax.broadcasted_iota(jnp.int32, (node_count, node_count), 0)
    column = lax.broadcasted_iota(jnp.int32, (node_count, node_count), 1)
    reached_ref[...] = jnp.where((parents_ref[...] == row) | (row == column), 1.0, 0.0)


def own_and_parents(parents):
    node_count = parents.shape[1]
    return pl.pallas_call(
        parent_kernel,
        out_shape=jax.ShapeDtypeStruct((node_count, node_count), jnp.float32),
        cost_estimate=pl.CostEstimate(flops=23070000000, bytes_accessed=8192, transcendentals=0),
    )(parents)


def ancestry(reached):
    for doubling in range((reached.shape[0] - 1).bit_length()):
        reached = jnp.minimum(jnp.dot(reached, reached, preferred_element_type=jnp.float32), 1.0)
    return reached.T


def attend_local(
    queries, cached_key_rows, cached_value_rows, tree_key_rows, tree_value_rows, lengths, related
):
    request_count = lengths.shape[0]
    node_count = related.shape[0]
    slot_length = cached_key_rows.shape[1]
    kv_local = cached_key_rows.shape[2] // HEAD_SIZE
    query_group_count = queries.shape[1] // (kv_local * HEAD_SIZE)
    scaled = 1.0 / math.sqrt(HEAD_SIZE)
    tree_query_block = queries.reshape(
        request_count, node_count, kv_local, query_group_count, HEAD_SIZE
    )
    joined_key_block = cached_key_rows.reshape(request_count, slot_length, kv_local, HEAD_SIZE)
    joined_value_block = cached_value_rows.reshape(request_count, slot_length, kv_local, HEAD_SIZE)
    tree_key_block = tree_key_rows.reshape(request_count, node_count, kv_local, HEAD_SIZE)
    tree_value_block = tree_value_rows.reshape(request_count, node_count, kv_local, HEAD_SIZE)
    cache_scores = (
        jnp.einsum(
            "rnkgd,rpkd->rkgnp",
            tree_query_block,
            joined_key_block,
            preferred_element_type=jnp.float32,
        )
        * scaled
    )
    tree_scores = (
        jnp.einsum(
            "rnkgd,rmkd->rkgnm",
            tree_query_block,
            tree_key_block,
            preferred_element_type=jnp.float32,
        )
        * scaled
    )
    visible = jnp.arange(slot_length, dtype=jnp.int32)[None, :] < lengths[:, None]
    cache_scores = jnp.where(visible[:, None, None, None, :], cache_scores, -1e30)
    tree_scores = jnp.where(related[None, None, None] > 0.5, tree_scores, -1e30)
    highest = jnp.maximum(jnp.max(cache_scores, axis=-1), jnp.max(tree_scores, axis=-1))[..., None]
    cache_raised = jnp.exp(cache_scores - highest)
    tree_raised = jnp.exp(tree_scores - highest)
    denominator = jnp.sum(cache_raised, axis=-1, keepdims=True) + jnp.sum(
        tree_raised, axis=-1, keepdims=True
    )
    cache_weights = (cache_raised / denominator).astype(jnp.bfloat16)
    tree_weights = (tree_raised / denominator).astype(jnp.bfloat16)
    output = jnp.einsum(
        "rkgnp,rpkd->rnkgd", cache_weights, joined_value_block, preferred_element_type=jnp.float32
    )
    output = output + jnp.einsum(
        "rkgnm,rmkd->rnkgd", tree_weights, tree_value_block, preferred_element_type=jnp.float32
    )
    return output.reshape(request_count * node_count, -1).astype(jnp.bfloat16)


def on_device(
    hidden,
    routes,
    routing_weights,
    w_gate,
    w_up,
    w_down,
    norm_gain,
    key_projection_weight,
    value_projection_weight,
    queries,
    cached_key_rows,
    cached_value_rows,
    lengths,
    parents,
):
    token_count = hidden.shape[0]
    top_count = routes.shape[1]
    expert_count = lax.axis_size("dp")
    capacity = min(token_count, 2 * token_count * top_count // expert_count)
    column_count = hidden.shape[1]
    to_opposite = around(w_down[0], 1, column_count)[3]
    routes, routing_weights, to_opposite = lax.optimization_barrier((routes, routing_weights, to_opposite))
    outgoing, both = routed_rows(routes, routing_weights, hidden, capacity)
    outgoing = outgoing.reshape(expert_count, capacity, column_count)
    outgoing, w_down = lax.optimization_barrier((outgoing, w_down))
    down_own, to_before, to_after, _ = around(w_down[0], 1, column_count)
    before, after, opposite = sent_around((to_before, to_after, to_opposite))
    opposite, parents = lax.optimization_barrier((opposite, parents))
    reached = own_and_parents(parents)
    hidden_units = w_gate.shape[2]
    both_weights = [
        jnp.concatenate(pair, axis=1)
        for pair in zip(around(w_gate[0], 0, column_count), around(w_up[0], 0, column_count))
    ]
    received = lax.all_to_all(outgoing, "dp", split_axis=0, concat_axis=0, tiled=True)
    received, before, after, opposite, both_weights, reached = lax.optimization_barrier(
        (received, before, after, opposite, both_weights, reached)
    )
    down_whole = jnp.concatenate([down_own, before, after, opposite], axis=0)
    related = ancestry(reached)
    down_blocks = jnp.split(down_whole, lax.axis_size("tp"))
    chunk = capacity // CHUNKS
    returned = []
    for part in range(CHUNKS):
        rows = received[:, part * chunk : (part + 1) * chunk].reshape(expert_count * chunk, column_count)
        products = summed_products(gathered_ring(rows), both_weights)
        gate_act, upward = products[:, :hidden_units], products[:, hidden_units:]
        active = (jax.nn.silu(gate_act) * upward).astype(jnp.bfloat16)
        made = summed_products([active, *sent_around([active] * 3)], down_blocks).astype(jnp.bfloat16)
        returned.append(
            lax.all_to_all(
                made.reshape(expert_count, chunk, column_count), "dp", split_axis=0, concat_axis=0, tiled=True
            )
        )
    flat_back = jnp.concatenate(returned, axis=1).reshape(expert_count * capacity, column_count)
    mixed = lax.dot_general(
        both, flat_back, (((0,), (0,)), ((), ())), preferred_element_type=jnp.float32
    )
    expert_mix = mixed[:token_count] + mixed[token_count:]
    own_out = (hidden.astype(jnp.float32) + expert_mix).astype(jnp.bfloat16)
    full_out = gathered_copies(own_out, "tp", 1)
    widened = full_out.astype(jnp.float32)
    scaling = lax.rsqrt(jnp.mean(widened * widened, axis=1, keepdims=True) + 1e-06)
    normed = (widened * scaling * norm_gain).astype(jnp.bfloat16)
    tree_key_rows = jnp.dot(
        normed, key_projection_weight, preferred_element_type=jnp.float32
    ).astype(jnp.bfloat16)
    tree_value_rows = jnp.dot(
        normed, value_projection_weight, preferred_element_type=jnp.float32
    ).astype(jnp.bfloat16)
    attended = attend_local(
        queries,
        cached_key_rows,
        cached_value_rows,
        tree_key_rows,
        tree_value_rows,
        lengths,
        related,
    )
    return (own_out, tree_key_rows, tree_value_rows, attended)


def solution(mesh):
    return jax.shard_map(
        on_device,
        mesh=mesh,
        in_specs=(
            P("dp", "tp"),
            P("dp", None),
            P("dp", None),
            P("dp", None, "tp"),
            P("dp", None, "tp"),
            P("dp", "tp", None),
            P(),
            P(None, "tp"),
            P(None, "tp"),
            P("dp", "tp"),
            P("dp", None, "tp"),
            P("dp", None, "tp"),
            P("dp"),
            P("dp", None),
        ),
        out_specs=(P("dp", "tp"), P("dp", "tp"), P("dp", "tp"), P("dp", "tp")),
        check_vma=False,
    )
```
